32 devices in a mesh: req: 4 (over z), row: 4 (over x, core), col: 2 (over y).
Axes of the slice: x: 2, y: 2, z: 4, core: 2. Of those that a mesh axis runs over, the one named last changes fastest.
Arguments:
- tokens: bfloat16 [1792, 4096], P('col', ('req', 'row')), may hold values from -6 to 6
- qkv_weight: bfloat16 [1792, 2304], P('col', 'row'), may hold values from -0.125 to 0.125
- out_weight: bfloat16 [1792, 1792], P('row', 'col'), may hold values from -0.125 to 0.125
- head_gain: float32 [1792], P('row'), may hold values from 0.1 to 1.9
- prefix_keys: bfloat16 [12, 256, 8192], P('req', 'row', 'col'), may hold values from -6 to 6
- prefix_values: bfloat16 [12, 1792, 8192], P('req', 'row', 'col'), may hold values from -6 to 6
- suffix_len: int32 [8], P(('req', 'col')), may hold values from 1 to 512, 3072 in all
- prefix_owner: int32 [8], P(('req', 'col')), may hold values from 0 to 11
Outputs:
- layer_out: bfloat16 [1792, 4096], P('col', ('req', 'row'))
The draws below stay inside these ranges and needn't reach their ends.
Inputs may be any that keep to these rules, and one draw needn't show every extreme that they name: `suffix_len`: the longest suffix has exactly 512 live tokens.
All inputs are finite; a program needn't handle non-finite values. No bound on the sum of `suffix_len` on one device may be relied on, other than what follows from the above.
Results may differ from the reference program's by a relative error of at most 0.015.
Values may be sent and summed in bfloat16 or wider, within the bound.
A program may use at most 128 MiB of HBM per device.

```python
import math
import jax
import jax.numpy as jnp
import numpy as np
from jax import lax

D = 1792
H = 16
FEAT = 16
PLEN = 8192
SLOTS = 512
HD = 112
PREFIXES = 12
REQS = 8
TOKENS = 4096
N_ROW = 4
N_COL = 2


def plant(drawn, key, low, high):
    longest = drawn.shape.index(max(drawn.shape))
    spots = []
    for shift in (0, 1):
        where = [jax.random.randint(jax.random.fold_in(key, axis), (), 0, length) for axis, length in enumerate(drawn.shape)]
        where[longest] = (where[longest] + shift) % drawn.shape[longest]
        spots.append(tuple(where))
    return drawn.at[spots[0]].set(low).at[spots[1]].set(high)


def block_scale(stream_key, shape, shards, least, high):
    loudness, own = 1.0, jax.random.fold_in(stream_key, 6)
    for dim, parts in shards:
        heights = jnp.exp(jax.random.uniform(jax.random.fold_in(own, dim), (parts,), jnp.float32, least / len(shards), high / len(shards)))
        loudness = loudness * jnp.repeat(heights, shape[dim] // parts).reshape([-1 if axis == dim else 1 for axis in range(len(shape))])
    return loudness


def split_up(amount, total, reach, lean):
    weights = [(1 << 20) // math.isqrt(standing ** lean) + 1 for standing in range(2, amount + 1)]
    spare, counts = total - reach - (amount - 1), [1] * (amount - 1)
    while spare > 0:
        candidates = [i for i in range(amount - 1) if counts[i] < reach]
        whole, remaining = sum([weights[i] for i in candidates]), spare
        for i in candidates:
            extra = min(reach - counts[i], max(1, remaining * weights[i] // whole), spare)
            counts[i] = counts[i] + extra
            spare = spare - extra
    return np.array([reach] + counts)


def ragged_sizes(rng, amount, total, limit, slope):
    if amount == 2:
        one = jax.random.randint(rng, (), max(1, total - limit), min(limit, total - 1) + 1)
        return jnp.stack([one, total - one])
    sizes = jnp.asarray(split_up(amount, total, limit, slope), jnp.int32)
    couples = (amount - 1) // 2
    giver, sink = sizes[1:1 + 2 * couples:2], sizes[2:2 + 2 * couples:2]
    slack = jnp.minimum(giver - 1, limit - sink)
    moved = jax.random.randint(jax.random.fold_in(rng, 1), (couples,), 0, 1 << 20) % (slack + 1)
    sizes = sizes.at[1:1 + 2 * couples:2].set(giver - moved).at[2:2 + 2 * couples:2].set(sink + moved)
    return sizes[jax.random.permutation(jax.random.fold_in(rng, 2), amount)]


def noise(own_key, extent, width, reach, cuts=(), held_as=jnp.bfloat16):
    gain = block_scale(own_key, extent, cuts, -0.22, 0.18) if cuts else 1.0
    drawn = jax.random.normal(own_key, extent, jnp.float32) * width * gain
    return jnp.minimum(jnp.maximum(drawn, -reach), reach).astype(held_as)


def setup_inputs(seed: int = 0) -> dict:
    keys = jax.random.split(jax.random.key(seed), 9)
    return {
        "tokens": noise(keys[0], (D, TOKENS), 1.0, 6.0, ((0, 2), (1, 16))),
        "qkv_weight": noise(keys[1], (D, H * (2 * FEAT + HD)), D ** -0.5, 0.125, ((0, 2), (1, 4))),
        "out_weight": noise(keys[2], (D, D), D ** -0.5, 0.125, ((0, 4), (1, 2))),
        "head_gain": jnp.clip(1.0 + 0.18 * jax.random.normal(keys[3], (D,), jnp.float32), 0.1, 1.9),
        "prefix_keys": noise(keys[4], (PREFIXES, H * FEAT, PLEN), 1.0, 6.0, ((0, 4), (1, 4), (2, 2))),
        "prefix_values": noise(keys[5], (PREFIXES, D, PLEN), 1.0, 6.0, ((0, 4), (1, 4), (2, 2))),
        "suffix_len": ragged_sizes(keys[6], REQS, REQS * SLOTS * 3 // 4, SLOTS, 2).astype(jnp.int32),
        "prefix_owner": plant(jax.random.randint(keys[7], (REQS,), 0, PREFIXES), jax.random.fold_in(keys[7], 1), 0, PREFIXES - 1).astype(jnp.int32),
    }


epsilon = 1e-05

def feature_map(values_in):
    feature_count = values_in.shape[-1]
    squares = (values_in[..., :, None] * values_in[..., None, :]).reshape(values_in.shape[:-1] + (feature_count * feature_count,))
    constant = jnp.ones(values_in.shape[:-1] + (1,), jnp.float32)
    linear = values_in * feature_count ** (-0.25)
    quadratic = squares * (0.5 ** 0.5 / feature_count ** 0.5)
    return jnp.concatenate([constant, linear, quadratic], axis=-1).astype(jnp.bfloat16)

def feature_columns(values_in):
    feature_count = values_in.shape[-2]
    length = values_in.shape[-1]
    squares = (values_in[..., :, None, :] * values_in[..., None, :, :]).reshape(values_in.shape[:-2] + (feature_count * feature_count, length))
    constant = jnp.ones(values_in.shape[:-2] + (1, length), jnp.float32)
    linear = values_in * feature_count ** (-0.25)
    quadratic = squares * (0.5 ** 0.5 / feature_count ** 0.5)
    return jnp.concatenate([constant, linear, quadratic], axis=-2).astype(jnp.bfloat16)

def reference(tokens, qkv_weight, out_weight, head_gain, prefix_keys, prefix_values, suffix_len, prefix_owner):
    row_width = 2 * FEAT + HD
    block_width = D // N_COL
    token_rows = tokens.T
    summed = jnp.zeros((TOKENS, H * row_width), jnp.float32)
    for column_index in range(N_COL):
        partial_sum = jnp.dot(token_rows[:, column_index * block_width:(column_index + 1) * block_width], qkv_weight[column_index * block_width:(column_index + 1) * block_width], preferred_element_type=jnp.float32)
        summed = summed + lax.optimization_barrier(partial_sum.astype(jnp.bfloat16)).astype(jnp.float32)
    projected = summed.astype(jnp.bfloat16).reshape(REQS, SLOTS, H, row_width)

    def one_state(cache_pair):
        keys_cached, values_cached = cache_pair
        feats = feature_columns(keys_cached.reshape(H, FEAT, PLEN).astype(jnp.float32))
        return jnp.einsum('het,hvt->hev', feats.astype(jnp.float32), values_cached.reshape(H, HD, PLEN).astype(jnp.float32))
    states = lax.map(one_state, (prefix_keys, prefix_values))
    gains = head_gain.reshape(H, HD).astype(jnp.float32)

    def one_request(request_item):
        block_rows, length, prefix_pick = request_item
        queries = block_rows[..., :FEAT]
        keys_now = block_rows[..., FEAT:2 * FEAT]
        values_now = block_rows[..., 2 * FEAT:]
        chosen = lax.dynamic_index_in_dim(states, prefix_pick, 0, keepdims=False)
        feats_query = feature_map(queries.astype(jnp.float32)).astype(jnp.float32)
        carried = jnp.einsum('the,hev->thv', feats_query, chosen, precision=lax.Precision.HIGHEST)
        scores = jnp.einsum('thf,shf->hts', queries.astype(jnp.float32), keys_now.astype(jnp.float32))
        weights = 1.0 + scores * FEAT ** (-0.5) + scores * scores * (0.5 / FEAT)
        positions = jnp.arange(SLOTS, dtype=jnp.int32)
        allowed = (positions[None, :] <= positions[:, None]) & (positions[None, :] < length)
        weights = jnp.where(allowed[None], weights, 0.0).astype(jnp.bfloat16)
        within = jnp.einsum('hts,shv->thv', weights.astype(jnp.float32), values_now.astype(jnp.float32))
        active = (positions < length)[:, None, None]
        attended = jnp.where(active, carried + within, 0.0)
        inverse_rms = lax.rsqrt(lax.optimization_barrier(jnp.mean(attended * attended, axis=-1, keepdims=True)) + epsilon)
        normed = attended * inverse_rms * gains
        return normed.astype(jnp.bfloat16).reshape(SLOTS, D)
    hidden = lax.map(one_request, (projected, suffix_len, prefix_owner)).reshape(TOKENS, D)
    row_block = D // N_ROW
    result = token_rows.astype(jnp.float32)
    for row_index in range(N_ROW):
        partial_sum = jnp.dot(hidden[:, row_index * row_block:(row_index + 1) * row_block], out_weight[row_index * row_block:(row_index + 1) * row_block], preferred_element_type=jnp.float32)
        result = result + lax.optimization_barrier(partial_sum.astype(jnp.bfloat16)).astype(jnp.float32)
    return result.astype(jnp.bfloat16).T
```

```python
import functools

import jax
import jax.numpy as jnp
from jax import lax
from jax.experimental import pallas as pl
from jax.experimental.pallas import tpu as pltpu
from jax.sharding import PartitionSpec as P

FEAT = 16
SLOTS = 512
HD = 112
NF = 160
epsilon = 1e-05
MESH = pl.DeviceIdType.MESH
BF = jnp.bfloat16
F32 = jnp.float32


def products(u, linear, diag, cross, const):
    parts = [(u * linear).astype(BF), (u * u * diag).astype(BF)]
    left = u * cross
    for s in range(1, 8):
        rolled = jnp.concatenate([u[s:], u[:s]], axis=0)
        parts.append((left * rolled).astype(BF))
    last = jnp.concatenate([left[:8] * u[8:], jnp.full((8, u.shape[1]), const, F32)], axis=0)
    parts.append(last.astype(BF))
    return jnp.concatenate(parts, axis=0)


def body(dims, tok_ref, qkv_ref, wo_ref, gain_ref, keys_ref, vals_ref, len_ref, own_ref, out_ref,
         tok_all, wo_all, qkv_t, wo_t, keys_v, vals_v, own_part, send_part, recv_part, proj,
         st_part, st_recv, sel, sel_recv, own_all, nrm, hid,
         ld_k, ld_v, tok_s, tok_r, wo_s, wo_r, part_s, part_r, st_s, st_r, sel_s, sel_r, ow_s, ow_r,
         nrm_s, nrm_r, hid_s, hid_r):
    n_req, n_row, n_col = dims
    n_x = n_row // 2
    z, rho, y = lax.axis_index("req"), lax.axis_index("row"), lax.axis_index("col")
    x, c = rho // 2, rho % 2
    mate = x * 2 + (1 - c)
    heads = wo_ref.shape[0] // HD
    width = 2 * FEAT + HD
    tr = tok_ref.shape[1]
    halves = SLOTS // tr
    n_pref, _, t_len = keys_ref.shape

    loads = []
    for h in range(heads):
        a = pltpu.make_async_copy(keys_ref.at[:, pl.ds(h * FEAT, FEAT)], keys_v.at[h], ld_k.at[h])
        b = pltpu.make_async_copy(vals_ref.at[:, pl.ds(h * HD, HD)], vals_v.at[h], ld_v.at[h])
        a.start()
        b.start()
        loads.append((a, b))

    barrier = pltpu.get_barrier_semaphore()
    for d in range(1, n_row):
        pl.semaphore_signal(barrier, inc=1, device_id=(z, (rho + d) % n_row, y), device_id_type=MESH)
    for d in range(1, n_col):
        pl.semaphore_signal(barrier, inc=1, device_id=(z, rho, (y + d) % n_col), device_id_type=MESH)
    for d in range(1, n_req):
        pl.semaphore_signal(barrier, inc=1, device_id=((z + d) % n_req, rho, y), device_id_type=MESH)

    qkv_t[...] = qkv_ref[...].T
    pl.semaphore_wait(barrier, n_row + n_col + n_req - 3)

    def remote(src, dst, s, r, dev):
        return pltpu.make_async_remote_copy(src_ref=src, dst_ref=dst, send_sem=s, recv_sem=r,
                                            device_id=dev, device_id_type=MESH)

    sent = []

    def send(*args):
        copy = remote(*args)
        copy.start()
        sent.append(copy)

    def spread(src, dst, ss, rs):
        for d in range(1, n_x):
            send(src, dst.at[2 * d], ss.at[2 * d], rs.at[2 * d], (z, ((x + d) % n_x) * 2 + c, y))
        send(src, dst.at[1], ss.at[1], rs.at[1], (z, mate, y))

    def forward(dst, ss, rs, d):
        remote(dst.at[2 * d], dst.at[2 * d], ss.at[2 * d], rs.at[2 * d], (z, mate, y)).wait_recv()
        send(dst.at[2 * d], dst.at[2 * d + 1], ss.at[2 * d + 1], rs.at[2 * d + 1], (z, mate, y))

    def arrived(dst, ss, rs, slot):
        remote(dst.at[slot], dst.at[slot], ss.at[slot], rs.at[slot], (z, mate, y)).wait_recv()

    def slot_row(slot):
        d, s = slot // 2, slot % 2
        return ((x - d + n_x) % n_x) * 2 + (c if s == 0 else 1 - c)

    spread(tok_ref, tok_all, tok_s, tok_r)
    for d in range(1, n_req):
        send(own_ref, own_all.at[d], ow_s.at[d], ow_r.at[d], ((z + d) % n_req, rho, y))

    def part_copy(slot):
        row = slot_row(slot)
        g = row * tr // SLOTS
        j = row % halves
        d = (g - y + n_col) % n_col
        k = (d - 1 + n_col) % n_col
        return g, j, remote(send_part.at[slot], recv_part.at[k, j], part_s.at[slot], part_r.at[k, j], (z, rho, g))

    def project(slot):
        tokens = tok_ref[...] if slot == 0 else tok_all[slot]
        value = jnp.dot(qkv_t[...], tokens, preferred_element_type=F32).astype(BF)
        g, j, copy = part_copy(slot)

        @pl.when(g == y)
        def _():
            own_part[j] = value

        @pl.when(g != y)
        def _():
            send_part[slot] = value
            copy.start()

    project(0)
    arrived(tok_all, tok_s, tok_r, 1)
    project(1)
    spread(wo_ref, wo_all, wo_s, wo_r)

    step = min(1024, t_len)

    def state(h):
        loads[h][0].wait()
        loads[h][1].wait()

        def one(p, carry):
            total = jnp.zeros((HD, NF), F32)
            for t in range(0, t_len, step):
                u = keys_v[h, p, :, t:t + step].astype(F32)
                feats = products(u, 1.0, 1.0, 1.0, 1.0)
                total += lax.dot_general(vals_v[h, p, :, t:t + step], feats, (((1,), (1,)), ((), ())),
                                         preferred_element_type=F32)
            st_part[h, p] = total.astype(BF)
            return carry

        lax.fori_loop(0, n_pref, one, 0)
        for d in range(1, n_col):
            send(st_part.at[h], st_recv.at[d, h], st_s.at[d, h], st_r.at[d, h], (z, rho, (y + d) % n_col))

    def choose(h):
        if h == 0:
            for d in range(1, n_req):
                remote(own_ref, own_all.at[d], ow_s.at[d], ow_r.at[d], (z, rho, y)).wait_recv()
        for d in range(1, n_col):
            remote(st_part.at[h], st_recv.at[d, h], st_s.at[d, h], st_r.at[d, h], (z, rho, y)).wait_recv()
        sums = []
        for p in range(n_pref):
            total = st_part[h, p].astype(F32)
            for d in range(1, n_col):
                total += st_recv[d, h, p].astype(F32)
            sums.append(total)
        for d in list(range(1, n_req)) + [0]:
            k = (n_req - d) % n_req
            owner = own_ref[0:1, 0:NF] if k == 0 else own_all[k, 0:1, 0:NF]
            value = jnp.zeros((HD, NF), F32)
            for p in range(n_pref):
                value = jnp.where(owner == z * n_pref + p, sums[p], value)
            sel[d, h] = value.astype(BF)
            if d:
                send(sel.at[d, h], sel_recv.at[d, h], sel_s.at[d, h], sel_r.at[d, h], ((z + d) % n_req, rho, y))

    half = max(1, heads // 2)
    for h in range(heads):
        state(h)
        if h > 0:
            choose(h - 1)
        if h == half - 1:
            for d in range(1, n_x):
                forward(tok_all, tok_s, tok_r, d)
        if h == half:
            for d in range(1, n_x):
                project(2 * d)
                arrived(tok_all, tok_s, tok_r, 2 * d + 1)
                project(2 * d + 1)
    choose(heads - 1)
    for d in range(1, n_x):
        forward(wo_all, wo_s, wo_r, d)

    for j in range(halves):
        total = own_part[j].astype(F32)
        for d in range(1, n_col):
            k = d - 1
            remote(send_part.at[0], recv_part.at[k, j], part_s.at[0], part_r.at[k, j], (z, rho, y)).wait_recv()
            total += recv_part[k, j].astype(F32)
        proj[:, j * tr:(j + 1) * tr] = total.astype(BF)

    def hid_copy(d, h, j):
        row = ((y - d + n_col) % n_col) * halves + j
        cols = pl.ds(h * HD, HD)
        return row, remote(nrm.at[d, h, j], hid.at[rho, cols], hid_s.at[d, h, j], hid_r.at[rho, h], (z, row, y))

    def scatter(d, h):
        for j in range(halves):
            row, copy = hid_copy(d, h, j)

            @pl.when(row == rho)
            def _():
                hid[rho, h * HD:(h + 1) * HD] = nrm[d, h, j]

            @pl.when(row != rho)
            def _():
                copy.start()

    def pass_on(h):
        for d in range(1, n_col):
            remote(nrm.at[0, h], nrm.at[d, h], nrm_s.at[d, h], nrm_r.at[d, h], (z, rho, y)).wait_recv()
            scatter(d, h)

    tile = min(tr, 256)
    live = len_ref[0:1, :]
    for h in range(heads):
        base = h * width
        q = proj[base:base + FEAT].astype(F32)
        k_rows = proj[base + FEAT:base + 2 * FEAT].astype(F32).T.astype(BF)
        v = proj[base + 2 * FEAT:base + width]
        pos = lax.broadcasted_iota(jnp.int32, (HD, SLOTS), 1)
        active = pos < live
        v = jnp.where(active, v.astype(F32), 0.0).astype(BF)
        for d in range(1, n_req):
            remote(sel.at[d, h], sel_recv.at[d, h], sel_s.at[d, h], sel_r.at[d, h], (z, rho, y)).wait_recv()
        s_t = sel[0, h].astype(F32)
        for d in range(1, n_req):
            s_t += sel_recv[d, h].astype(F32)
        feats = products(q, 0.25, 1.0 / 32, 1.0 / 16, 0.125)
        carried = jnp.dot(s_t.astype(BF), feats, preferred_element_type=F32)
        for t in range(0, SLOTS, tile):
            keep = t + tile
            scores = jnp.dot(k_rows[:keep], q[:, t:keep].astype(BF), preferred_element_type=F32)
            weights = 1.0 + scores * 0.25 + scores * scores * (0.5 / FEAT)
            si = lax.broadcasted_iota(jnp.int32, (keep, tile), 0)
            ti = lax.broadcasted_iota(jnp.int32, (keep, tile), 1) + t
            weights = jnp.where(si <= ti, weights, 0.0).astype(BF)
            att = carried[:, t:keep] + jnp.dot(v[:, :keep], weights, preferred_element_type=F32)
            att = jnp.where(active[:, t:keep], att, 0.0)
            inv = lax.rsqrt(jnp.mean(att * att, axis=0, keepdims=True) + epsilon)
            normed = (att * inv * gain_ref[h * HD:(h + 1) * HD, :]).astype(BF)
            j, o = t // tr, t % tr
            nrm[0, h, j, :, o:o + tile] = normed
        for d in range(1, n_col):
            send(nrm.at[0, h], nrm.at[d, h], nrm_s.at[d, h], nrm_r.at[d, h], (z, rho, (y + d) % n_col))
        scatter(0, h)
        if h > 0:
            pass_on(h - 1)
    wo_t[0] = wo_ref[...].T
    pass_on(heads - 1)
    for slot in range(1, n_row):
        if slot == 1 or slot % 2:
            arrived(wo_all, wo_s, wo_r, slot)
        wo_t[slot] = wo_all[slot].T

    for k in range(1, n_row):
        src = (rho + k) % n_row
        for h in range(heads):
            cols = pl.ds(h * HD, HD)
            remote(nrm.at[0, h, 0], hid.at[src, cols], hid_s.at[0, h, 0], hid_r.at[src, h], (z, rho, y)).wait_recv()

    total = tok_ref[...].astype(F32)
    for slot in range(n_row):
        total += jnp.dot(wo_t[slot], hid[slot_row(slot)], preferred_element_type=F32)
    out_ref[...] = total.astype(BF)

    for copy in sent:
        copy.wait_send()
    for slot in range(n_row):
        g, _, copy = part_copy(slot)

        @pl.when(g != y)
        def _():
            copy.wait_send()
    for d in range(n_col):
        for h in range(heads):
            for j in range(halves):
                row, copy = hid_copy(d, h, j)

                @pl.when(row != rho)
                def _():
                    copy.wait_send()


def shards(dims, tokens, qkv_weight, out_weight, head_gain, prefix_keys, prefix_values, suffix_len, prefix_owner):
    n_req, n_row, n_col = dims
    dk, tr = tokens.shape
    rows, wide = out_weight.shape
    heads = rows // HD
    halves = SLOTS // tr
    qkv = qkv_weight.shape[1]
    n_pref, _, t_len = prefix_keys.shape
    lens = jnp.broadcast_to(suffix_len[:, None], (8, SLOTS))
    owners = jnp.broadcast_to(prefix_owner[:, None], (8, 256))
    vm = pltpu.VMEM
    dma = pltpu.SemaphoreType.DMA
    scratch = [
        vm((n_row, dk, tr), BF), vm((n_row, rows, wide), BF), vm((qkv, dk), BF), vm((n_row, wide, rows), BF),
        vm((heads, n_pref, FEAT, t_len), BF), vm((heads, n_pref, HD, t_len), BF),
        vm((halves, qkv, tr), BF), vm((n_row, qkv, tr), BF), vm((n_col, halves, qkv, tr), BF), vm((qkv, SLOTS), BF),
        vm((heads, n_pref, HD, NF), BF), vm((n_col, heads, n_pref, HD, NF), BF),
        vm((n_req, heads, HD, NF), BF), vm((n_req, heads, HD, NF), BF), vm((n_req, 8, 256), jnp.int32),
        vm((n_col, heads, halves, HD, tr), BF), vm((n_row, rows, tr), BF),
        dma((heads,)), dma((heads,)), dma((n_row,)), dma((n_row,)), dma((n_row,)), dma((n_row,)),
        dma((n_row,)), dma((n_col, halves)), dma((n_col, heads)), dma((n_col, heads)),
        dma((n_req, heads)), dma((n_req, heads)), dma((n_req,)), dma((n_req,)),
        dma((n_col, heads)), dma((n_col, heads)), dma((n_col, heads, halves)), dma((n_row, heads)),
    ]
    here = pl.BlockSpec(memory_space=pltpu.VMEM)
    far = pl.BlockSpec(memory_space=pl.ANY)
    return pl.pallas_call(
        functools.partial(body, dims),
        out_shape=jax.ShapeDtypeStruct(tokens.shape, BF),
        in_specs=[here, here, here, here, far, far, here, here],
        out_specs=here,
        scratch_shapes=scratch,
        compiler_params=pltpu.CompilerParams(collective_id=0, has_side_effects=True,
                                             vmem_limit_bytes=60 * 1024 * 1024),
    )(tokens, qkv_weight, out_weight, head_gain[:, None], prefix_keys, prefix_values, lens, owners)


def solution(mesh):
    in_specs = (
        P("col", ("req", "row")),
        P("col", "row"),
        P("row", "col"),
        P("row"),
        P("req", "row", "col"),
        P("req", "row", "col"),
        P(("req", "col")),
        P(("req", "col")),
    )
    out_specs = P("col", ("req", "row"))
    dims = (mesh.shape["req"], mesh.shape["row"], mesh.shape["col"])
    return jax.shard_map(functools.partial(shards, dims), mesh=mesh, in_specs=in_specs, out_specs=out_specs,
                         check_vma=False)
```

```python
import functools

import jax
import jax.numpy as jnp
from jax import lax
from jax.experimental import pallas as pl
from jax.experimental.pallas import tpu as pltpu
from jax.sharding import PartitionSpec as P

FEAT = 16
SLOTS = 512
HD = 112
NF = 160
epsilon = 1e-05
MESH = pl.DeviceIdType.MESH
BF = jnp.bfloat16
F32 = jnp.float32


def products(u, linear, diag, cross, const):
    parts = [(u * linear).astype(BF), (u * u * diag).astype(BF)]
    left = u * cross
    for s in range(1, 8):
        rolled = jnp.concatenate([u[s:], u[:s]], axis=0)
        parts.append((left * rolled).astype(BF))
    last = jnp.concatenate([left[:8] * u[8:], jnp.full((8, u.shape[1]), const, F32)], axis=0)
    parts.append(last.astype(BF))
    return jnp.concatenate(parts, axis=0)


def body(dims, tok_any, qkv_any, wo_any, gain_ref, keys_ref, vals_ref, len_ref, own_ref, out_ref,
         tok_ref, wo_ref, gain_c, inner, tok_all, wo_all, qkv_t, wo_t, keys_v, vals_v, own_part, send_part, recv_part, proj,
         st_part, st_recv, sel, sel_recv, own_all, nrm, hid,
         ld_w, ld_k, ld_v, tok_s, tok_r, wo_s, wo_r, part_s, part_r, st_s, st_r, sel_s, sel_r, ow_s, ow_r,
         nrm_s, nrm_r, hid_s, hid_r):
    n_req, n_row, n_col = dims
    n_x = n_row // 2
    z, rho, y = lax.axis_index("req"), lax.axis_index("row"), lax.axis_index("col")
    x, c = rho // 2, rho % 2
    mate = x * 2 + (1 - c)
    heads = wo_ref.shape[0] // HD
    width = 2 * FEAT + HD
    tr = tok_ref.shape[1]
    halves = SLOTS // tr
    n_pref, _, t_len = keys_ref.shape

    first = [pltpu.make_async_copy(tok_any, tok_ref, ld_w.at[0]),
             pltpu.make_async_copy(qkv_any, qkv_t, ld_w.at[1]),
             pltpu.make_async_copy(wo_any, wo_ref, ld_w.at[2])]
    first[0].start()
    first[1].start()
    loads = []
    for h in range(heads):
        a = pltpu.make_async_copy(keys_ref.at[:, pl.ds(h * FEAT, FEAT)], keys_v.at[h], ld_k.at[h])
        b = pltpu.make_async_copy(vals_ref.at[:, pl.ds(h * HD, HD)], vals_v.at[h], ld_v.at[h])
        a.start()
        b.start()
        loads.append((a, b))
    first[2].start()

    barrier = pltpu.get_barrier_semaphore()
    for d in range(1, n_row):
        pl.semaphore_signal(barrier, inc=1, device_id=(z, (rho + d) % n_row, y), device_id_type=MESH)
    for d in range(1, n_col):
        pl.semaphore_signal(barrier, inc=1, device_id=(z, rho, (y + d) % n_col), device_id_type=MESH)
    for d in range(1, n_req):
        pl.semaphore_signal(barrier, inc=1, device_id=((z + d) % n_req, rho, y), device_id_type=MESH)

    own_all[0] = jnp.full((8, 128), own_ref[0], jnp.int32)
    gain_c[...] = jnp.broadcast_to(gain_ref[...], (8, gain_ref.shape[1])).T
    first[0].wait()
    pl.semaphore_wait(barrier, n_row + n_col + n_req - 3)

    def remote(src, dst, s, r, dev):
        return pltpu.make_async_remote_copy(src_ref=src, dst_ref=dst, send_sem=s, recv_sem=r,
                                            device_id=dev, device_id_type=MESH)

    sent = []

    def send(*args):
        copy = remote(*args)
        copy.start()
        sent.append(copy)

    def spread(src, dst, ss, rs):
        for d in range(1, n_x):
            send(src, dst.at[2 * d], ss.at[2 * d], rs.at[2 * d], (z, ((x + d) % n_x) * 2 + c, y))
        send(src, dst.at[1], ss.at[1], rs.at[1], (z, mate, y))

    def forward(dst, ss, rs, d):
        remote(dst.at[2 * d], dst.at[2 * d], ss.at[2 * d], rs.at[2 * d], (z, mate, y)).wait_recv()
        send(dst.at[2 * d], dst.at[2 * d + 1], ss.at[2 * d + 1], rs.at[2 * d + 1], (z, mate, y))

    def arrived(dst, ss, rs, slot):
        remote(dst.at[slot], dst.at[slot], ss.at[slot], rs.at[slot], (z, mate, y)).wait_recv()

    def slot_row(slot):
        d, s = slot // 2, slot % 2
        return ((x - d + n_x) % n_x) * 2 + (c if s == 0 else 1 - c)

    spread(tok_ref, tok_all, tok_s, tok_r)
    for d in range(1, n_req):
        send(own_all.at[0], own_all.at[d], ow_s.at[d], ow_r.at[d], ((z + d) % n_req, rho, y))

    def part_copy(slot):
        row = slot_row(slot)
        g = row * tr // SLOTS
        j = row % halves
        d = (g - y + n_col) % n_col
        k = (d - 1 + n_col) % n_col
        return g, j, remote(send_part.at[slot], recv_part.at[k, j], part_s.at[slot], part_r.at[k, j], (z, rho, g))

    def project(slot):
        tokens = tok_ref[...] if slot == 0 else tok_all[slot]
        value = jnp.dot(qkv_t[...], tokens, preferred_element_type=F32).astype(BF)
        g, j, copy = part_copy(slot)

        @pl.when(g == y)
        def _():
            own_part[j] = value

        @pl.when(g != y)
        def _():
            send_part[slot] = value
            copy.start()

    first[1].wait()
    project(0)
    arrived(tok_all, tok_s, tok_r, 1)
    project(1)

    step = min(1024, t_len)

    def state(h):
        loads[h][0].wait()
        loads[h][1].wait()

        def one(p, carry):
            total = jnp.zeros((NF, HD), F32)
            for t in range(0, t_len, step):
                u = keys_v[h, p, :, t:t + step].astype(F32)
                feats = products(u, 1.0, 1.0, 1.0, 1.0)
                total += lax.dot_general(feats, vals_v[h, p, :, t:t + step], (((1,), (1,)), ((), ())),
                                         preferred_element_type=F32)
            st_part[h, p] = total.astype(BF)
            return carry

        lax.fori_loop(0, n_pref, one, 0)
        for d in range(1, n_col):
            send(st_part.at[h], st_recv.at[d, h], st_s.at[d, h], st_r.at[d, h], (z, rho, (y + d) % n_col))

    def choose(h):
        if h == 0:
            for d in range(1, n_req):
                remote(own_all.at[0], own_all.at[d], ow_s.at[d], ow_r.at[d], (z, rho, y)).wait_recv()
        for d in range(1, n_col):
            remote(st_part.at[h], st_recv.at[d, h], st_s.at[d, h], st_r.at[d, h], (z, rho, y)).wait_recv()
        sums = []
        for p in range(n_pref):
            total = st_part[h, p].astype(F32)
            for d in range(1, n_col):
                total += st_recv[d, h, p].astype(F32)
            sums.append(total)
        for d in list(range(1, n_req)) + [0]:
            k = (n_req - d) % n_req
            owner = own_all[k, 0:1, 0:HD]
            value = jnp.zeros((NF, HD), F32)
            for p in range(n_pref):
                value = jnp.where(owner == z * n_pref + p, sums[p], value)
            sel[d, h] = value.astype(BF)
            if d:
                send(sel.at[d, h], sel_recv.at[d, h], sel_s.at[d, h], sel_r.at[d, h], ((z + d) % n_req, rho, y))

    half = max(1, heads // 2)
    for h in range(heads):
        state(h)
        if h > 0:
            choose(h - 1)
        if h == half:
            for d in range(1, n_x):
                forward(tok_all, tok_s, tok_r, d)
                project(2 * d)
            first[2].wait()
            spread(wo_ref, wo_all, wo_s, wo_r)
        if h == heads - 1:
            for d in range(1, n_x):
                arrived(tok_all, tok_s, tok_r, 2 * d + 1)
                project(2 * d + 1)
    choose(heads - 1)
    wo_t[0] = wo_ref[...].T

    for j in range(halves):
        total = own_part[j].astype(F32)
        for d in range(1, n_col):
            k = d - 1
            remote(send_part.at[0], recv_part.at[k, j], part_s.at[0], part_r.at[k, j], (z, rho, y)).wait_recv()
            total += recv_part[k, j].astype(F32)
        proj[:, j * tr:(j + 1) * tr] = total.astype(BF)

    def hid_copy(d, h, j):
        row = ((y - d + n_col) % n_col) * halves + j
        cols = pl.ds(h * HD, HD)
        return row, remote(nrm.at[d, h, j], hid.at[rho, cols], hid_s.at[d, h, j], hid_r.at[rho, h], (z, row, y))

    def scatter(d, h):
        for j in range(halves):
            row, copy = hid_copy(d, h, j)

            @pl.when(row == rho)
            def _():
                hid[rho, h * HD:(h + 1) * HD] = nrm[d, h, j]

            @pl.when(row != rho)
            def _():
                copy.start()

    def pass_on(h):
        for d in range(1, n_col):
            remote(nrm.at[0, h], nrm.at[d, h], nrm_s.at[d, h], nrm_r.at[d, h], (z, rho, y)).wait_recv()
            scatter(d, h)

    tile = min(tr, 256)
    live = len_ref[0]
    active = lax.broadcasted_iota(jnp.int32, (HD, SLOTS), 1) < live
    for h in range(heads):
        base = h * width
        q = proj[base:base + FEAT]
        k_rows = proj[base + FEAT:base + 2 * FEAT].astype(F32).T.astype(BF)
        v = proj[base + 2 * FEAT:base + width]
        v = jnp.where(active, v.astype(F32), 0.0).astype(BF)
        for t in range(0, SLOTS, tile):
            keep = t + tile
            scores = jnp.dot(k_rows[:keep], q[:, t:keep], preferred_element_type=F32)
            weights = 1.0 + scores * 0.25 + scores * scores * (0.5 / FEAT)
            si = lax.broadcasted_iota(jnp.int32, (keep, tile), 0)
            ti = lax.broadcasted_iota(jnp.int32, (keep, tile), 1) + t
            weights = jnp.where(si <= ti, weights, 0.0).astype(BF)
            inner[h, :, t:keep] = jnp.dot(v[:, :keep], weights, preferred_element_type=F32)

    for d in range(1, n_x):
        forward(wo_all, wo_s, wo_r, d)

    for h in range(heads):
        feats = products(proj[h * width:h * width + FEAT].astype(F32), 0.25, 1.0 / 32, 1.0 / 16, 0.125)
        for d in range(1, n_req):
            remote(sel.at[d, h], sel_recv.at[d, h], sel_s.at[d, h], sel_r.at[d, h], (z, rho, y)).wait_recv()
        state_h = sel[0, h].astype(F32)
        for d in range(1, n_req):
            state_h += sel_recv[d, h].astype(F32)
        att = inner[h] + jnp.dot(state_h.T.astype(BF), feats, preferred_element_type=F32)
        att = jnp.where(active, att, 0.0)
        inv = lax.rsqrt(jnp.mean(att * att, axis=0, keepdims=True) + epsilon)
        normed = (att * inv * gain_c[h * HD:(h + 1) * HD, 0:1]).astype(BF)
        for j in range(halves):
            nrm[0, h, j] = normed[:, j * tr:(j + 1) * tr]
        for d in range(1, n_col):
            send(nrm.at[0, h], nrm.at[d, h], nrm_s.at[d, h], nrm_r.at[d, h], (z, rho, (y + d) % n_col))
        scatter(0, h)
        if h > 0:
            pass_on(h - 1)
    pass_on(heads - 1)
    for slot in range(1, n_row):
        if slot == 1 or slot % 2:
            arrived(wo_all, wo_s, wo_r, slot)
        wo_t[slot] = wo_all[slot].T

    total = jnp.dot(wo_t[0], hid[rho], preferred_element_type=F32)
    for slot in range(1, n_row):
        src = slot_row(slot)
        for h in range(heads):
            cols = pl.ds(h * HD, HD)
            remote(nrm.at[0, h, 0], hid.at[src, cols], hid_s.at[0, h, 0], hid_r.at[src, h], (z, rho, y)).wait_recv()
        total += jnp.dot(wo_t[slot], hid[src], preferred_element_type=F32)
    out_ref[...] = total

    for copy in sent:
        copy.wait_send()
    for slot in range(n_row):
        g, _, copy = part_copy(slot)

        @pl.when(g != y)
        def _():
            copy.wait_send()
    for d in range(n_col):
        for h in range(heads):
            for j in range(halves):
                row, copy = hid_copy(d, h, j)

                @pl.when(row != rho)
                def _():
                    copy.wait_send()


def shards(dims, tokens, qkv_weight, out_weight, head_gain, prefix_keys, prefix_values, suffix_len, prefix_owner):
    n_req, n_row, n_col = dims
    dk, tr = tokens.shape
    rows, wide = out_weight.shape
    heads = rows // HD
    halves = SLOTS // tr
    qkv = qkv_weight.shape[1]
    n_pref, _, t_len = prefix_keys.shape
    vm = pltpu.VMEM
    dma = pltpu.SemaphoreType.DMA
    scratch = [
        vm((dk, tr), BF), vm((rows, wide), BF), vm((rows, 8), F32), vm((heads, HD, SLOTS), F32),
        vm((n_row, dk, tr), BF), vm((n_row, rows, wide), BF), vm((qkv, dk), BF), vm((n_row, wide, rows), BF),
        vm((heads, n_pref, FEAT, t_len), BF), vm((heads, n_pref, HD, t_len), BF),
        vm((halves, qkv, tr), BF), vm((n_row, qkv, tr), BF), vm((n_col, halves, qkv, tr), BF), vm((qkv, SLOTS), BF),
        vm((heads, n_pref, NF, HD), BF), vm((n_col, heads, n_pref, NF, HD), BF),
        vm((n_req, heads, NF, HD), BF), vm((n_req, heads, NF, HD), BF), vm((n_req, 8, 128), jnp.int32),
        vm((n_col, heads, halves, HD, tr), BF), vm((n_row, rows, tr), BF),
        dma((3,)), dma((heads,)), dma((heads,)), dma((n_row,)), dma((n_row,)), dma((n_row,)), dma((n_row,)),
        dma((n_row,)), dma((n_col, halves)), dma((n_col, heads)), dma((n_col, heads)),
        dma((n_req, heads)), dma((n_req, heads)), dma((n_req,)), dma((n_req,)),
        dma((n_col, heads)), dma((n_col, heads)), dma((n_col, heads, halves)), dma((n_row, heads)),
    ]
    here = pl.BlockSpec(memory_space=pltpu.VMEM)
    far = pl.BlockSpec(memory_space=pl.ANY)
    scalar = pl.BlockSpec(memory_space=pltpu.SMEM)
    mixed = pl.pallas_call(
        functools.partial(body, dims),
        out_shape=jax.ShapeDtypeStruct(tokens.shape, F32),
        in_specs=[far, far, far, here, far, far, scalar, scalar],
        out_specs=here,
        scratch_shapes=scratch,
        compiler_params=pltpu.CompilerParams(collective_id=0, has_side_effects=True,
                                             vmem_limit_bytes=60 * 1024 * 1024),
    )(tokens, qkv_weight.T, out_weight, head_gain[None, :], prefix_keys, prefix_values, suffix_len, prefix_owner)
    return (tokens.astype(F32) + mixed).astype(BF)


def solution(mesh):
    in_specs = (
        P("col", ("req", "row")),
        P("col", "row"),
        P("row", "col"),
        P("row"),
        P("req", "row", "col"),
        P("req", "row", "col"),
        P(("req", "col")),
        P(("req", "col")),
    )
    out_specs = P("col", ("req", "row"))
    dims = (mesh.shape["req"], mesh.shape["row"], mesh.shape["col"])
    return jax.shard_map(functools.partial(shards, dims), mesh=mesh, in_specs=in_specs, out_specs=out_specs,
                         check_vma=False)
```

```python
import functools

import jax
import jax.numpy as jnp
from jax import lax
from jax.experimental import pallas as pl
from jax.experimental.pallas import tpu as pltpu
from jax.sharding import PartitionSpec as P

FEAT = 16
SLOTS = 512
HD = 112
NF = 160
epsilon = 1e-05
MESH = pl.DeviceIdType.MESH
BF = jnp.bfloat16
F32 = jnp.float32


def products(u, linear, diag, cross, const):
    parts = [(u * linear).astype(BF), (u * u * diag).astype(BF)]
    left = u * cross
    for s in range(1, 8):
        parts.append((left * pltpu.roll(u, s, 0)).astype(BF))
    last = jnp.concatenate([left[:8] * u[8:], jnp.full((8, u.shape[1]), const, F32)], axis=0)
    parts.append(last.astype(BF))
    return jnp.concatenate(parts, axis=0)


def key_products(rows):
    u = rows.astype(F32)
    parts = [rows, rows * rows]
    for s in range(1, 8):
        parts.append(rows * pltpu.roll(u, s, 0).astype(BF))
    last = jnp.concatenate([u[:8] * u[8:], jnp.full((8, u.shape[1]), 1.0, F32)], axis=0)
    parts.append(last.astype(BF))
    return jnp.concatenate(parts, axis=0)


def body(dims, tok_any, qkv_any, wo_any, gain_ref, keys_ref, vals_ref, len_ref, own_ref, out_ref,
         tok_ref, wo_ref, gain_c, inner, tok_all, wo_all, qkv_t, wo_t, keys_v, vals_v, own_part, send_part, recv_part, proj,
         st_part, st_recv, sel, sel_recv, own_all, nrm, hid,
         ld_w, ld_k, ld_v, tok_s, tok_r, wo_s, wo_r, part_s, part_r, st_s, st_r, sel_s, sel_r, ow_s, ow_r,
         nrm_s, nrm_r, hid_s, hid_r):
    n_req, n_row, n_col = dims
    n_x = n_row // 2
    z, rho, y = lax.axis_index("req"), lax.axis_index("row"), lax.axis_index("col")
    x, c = rho // 2, rho % 2
    mate = x * 2 + (1 - c)
    heads = wo_ref.shape[0] // HD
    width = 2 * FEAT + HD
    tr = tok_ref.shape[1]
    halves = SLOTS // tr
    n_pref, _, t_len = keys_ref.shape

    first = [pltpu.make_async_copy(tok_any, tok_ref, ld_w.at[0]),
             pltpu.make_async_copy(qkv_any, qkv_t, ld_w.at[1]),
             pltpu.make_async_copy(wo_any, wo_ref, ld_w.at[2])]
    first[0].start()
    first[1].start()
    first[2].start()
    loads = []
    for h in range(heads):
        a = pltpu.make_async_copy(keys_ref.at[:, pl.ds(h * FEAT, FEAT)], keys_v.at[h], ld_k.at[h])
        b = pltpu.make_async_copy(vals_ref.at[:, pl.ds(h * HD, HD)], vals_v.at[h], ld_v.at[h])
        a.start()
        b.start()
        loads.append((a, b))

    barrier = pltpu.get_barrier_semaphore()
    for d in range(1, n_row):
        pl.semaphore_signal(barrier, inc=1, device_id=(z, (rho + d) % n_row, y), device_id_type=MESH)
    for d in range(1, n_col):
        pl.semaphore_signal(barrier, inc=1, device_id=(z, rho, (y + d) % n_col), device_id_type=MESH)
    for d in range(1, n_req):
        pl.semaphore_signal(barrier, inc=1, device_id=((z + d) % n_req, rho, y), device_id_type=MESH)

    own_all[0] = jnp.full((8, 128), own_ref[0], jnp.int32)
    gain_c[...] = jnp.broadcast_to(gain_ref[...], (8, gain_ref.shape[1])).T
    first[2].wait()
    wo_t[...] = wo_ref[...].T
    first[0].wait()
    pl.semaphore_wait(barrier, n_row + n_col + n_req - 3)

    def remote(src, dst, s, r, dev):
        return pltpu.make_async_remote_copy(src_ref=src, dst_ref=dst, send_sem=s, recv_sem=r,
                                            device_id=dev, device_id_type=MESH)

    sent = []

    def send(*args):
        copy = remote(*args)
        copy.start()
        sent.append(copy)

    def spread(src, dst, ss, rs):
        for d in range(1, n_x):
            send(src, dst.at[2 * d], ss.at[2 * d], rs.at[2 * d], (z, ((x + d) % n_x) * 2 + c, y))
        send(src, dst.at[1], ss.at[1], rs.at[1], (z, mate, y))

    def forward(dst, ss, rs, d):
        remote(dst.at[2 * d], dst.at[2 * d], ss.at[2 * d], rs.at[2 * d], (z, mate, y)).wait_recv()
        send(dst.at[2 * d], dst.at[2 * d + 1], ss.at[2 * d + 1], rs.at[2 * d + 1], (z, mate, y))

    def arrived(dst, ss, rs, slot):
        remote(dst.at[slot], dst.at[slot], ss.at[slot], rs.at[slot], (z, mate, y)).wait_recv()

    def slot_row(slot):
        d, s = slot // 2, slot % 2
        return ((x - d + n_x) % n_x) * 2 + (c if s == 0 else 1 - c)

    spread(tok_ref, tok_all, tok_s, tok_r)
    for d in range(1, n_req):
        send(own_all.at[0], own_all.at[d], ow_s.at[d], ow_r.at[d], ((z + d) % n_req, rho, y))

    def part_copy(slot):
        row = slot_row(slot)
        g = row * tr // SLOTS
        j = row % halves
        d = (g - y + n_col) % n_col
        k = (d - 1 + n_col) % n_col
        return g, j, remote(send_part.at[slot], recv_part.at[k, j], part_s.at[slot], part_r.at[k, j], (z, rho, g))

    def project(slot):
        tokens = tok_ref[...] if slot == 0 else tok_all[slot]
        value = jnp.dot(qkv_t[...], tokens, preferred_element_type=F32).astype(BF)
        g, j, copy = part_copy(slot)

        @pl.when(g == y)
        def _():
            own_part[j] = value

        @pl.when(g != y)
        def _():
            send_part[slot] = value
            copy.start()

    first[1].wait()
    project(0)
    arrived(tok_all, tok_s, tok_r, 1)
    project(1)

    step = min(1024, t_len)

    def state(h):
        loads[h][0].wait()
        loads[h][1].wait()

        def one(p, carry):
            total = jnp.zeros((NF, HD), F32)
            for t in range(0, t_len, step):
                feats = key_products(keys_v[h, p, :, t:t + step])
                total += lax.dot_general(feats, vals_v[h, p, :, t:t + step], (((1,), (1,)), ((), ())),
                                         preferred_element_type=F32)
            st_part[h, p] = total.astype(BF)
            return carry

        lax.fori_loop(0, n_pref, one, 0)
        for d in range(1, n_col):
            send(st_part.at[h], st_recv.at[d, h], st_s.at[d, h], st_r.at[d, h], (z, rho, (y + d) % n_col))

    def choose(h):
        if h == 0:
            for d in range(1, n_req):
                remote(own_all.at[0], own_all.at[d], ow_s.at[d], ow_r.at[d], (z, rho, y)).wait_recv()
        for d in range(1, n_col):
            remote(st_part.at[h], st_recv.at[d, h], st_s.at[d, h], st_r.at[d, h], (z, rho, y)).wait_recv()
        sums = []
        for p in range(n_pref):
            total = st_part[h, p].astype(F32)
            for d in range(1, n_col):
                total += st_recv[d, h, p].astype(F32)
            sums.append(total)
        for d in list(range(1, n_req)) + [0]:
            k = (n_req - d) % n_req
            owner = own_all[k, 0:1, 0:HD]
            value = jnp.zeros((NF, HD), F32)
            for p in range(n_pref):
                value = jnp.where(owner == z * n_pref + p, sums[p], value)
            sel[d, h] = value.astype(BF)
            if d:
                send(sel.at[d, h], sel_recv.at[d, h], sel_s.at[d, h], sel_r.at[d, h], ((z + d) % n_req, rho, y))

    half = max(1, heads // 2)
    for h in range(heads):
        state(h)
        if h > 0:
            choose(h - 1)
        if h == half:
            for d in range(1, n_x):
                forward(tok_all, tok_s, tok_r, d)
                project(2 * d)
            spread(wo_t, wo_all, wo_s, wo_r)
        if h == heads - 1:
            for d in range(1, n_x):
                arrived(tok_all, tok_s, tok_r, 2 * d + 1)
                project(2 * d + 1)
    choose(heads - 1)
    for j in range(halves):
        total = own_part[j].astype(F32)
        for d in range(1, n_col):
            k = d - 1
            remote(send_part.at[0], recv_part.at[k, j], part_s.at[0], part_r.at[k, j], (z, rho, y)).wait_recv()
            total += recv_part[k, j].astype(F32)
        proj[:, j * tr:(j + 1) * tr] = total.astype(BF)

    def hid_copy(d, h, j):
        row = ((y - d + n_col) % n_col) * halves + j
        cols = pl.ds(h * HD, HD)
        return row, remote(nrm.at[d, h, j], hid.at[rho, cols], hid_s.at[d, h, j], hid_r.at[rho, h], (z, row, y))

    def scatter(d, h):
        for j in range(halves):
            row, copy = hid_copy(d, h, j)

            @pl.when(row == rho)
            def _():
                hid[rho, h * HD:(h + 1) * HD] = nrm[d, h, j]

            @pl.when(row != rho)
            def _():
                copy.start()

    def pass_on(h):
        for d in range(1, n_col):
            remote(nrm.at[0, h], nrm.at[d, h], nrm_s.at[d, h], nrm_r.at[d, h], (z, rho, y)).wait_recv()
            scatter(d, h)

    tile = min(tr, 256)
    live = len_ref[0]
    active = lax.broadcasted_iota(jnp.int32, (HD, SLOTS), 1) < live
    for h in range(heads):
        base = h * width
        q = proj[base:base + FEAT]
        k_rows = proj[base + FEAT:base + 2 * FEAT].astype(F32).T.astype(BF)
        v = proj[base + 2 * FEAT:base + width]
        v = jnp.where(active, v.astype(F32), 0.0).astype(BF)
        for t in range(0, SLOTS, tile):
            keep = t + tile
            scores = jnp.dot(k_rows[:keep], q[:, t:keep], preferred_element_type=F32)
            weights = 1.0 + scores * 0.25 + scores * scores * (0.5 / FEAT)
            si = lax.broadcasted_iota(jnp.int32, (keep, tile), 0)
            ti = lax.broadcasted_iota(jnp.int32, (keep, tile), 1) + t
            weights = jnp.where(si <= ti, weights, 0.0).astype(BF)
            inner[h, :, t:keep] = jnp.dot(v[:, :keep], weights, preferred_element_type=F32)

    for d in range(1, n_x):
        forward(wo_all, wo_s, wo_r, d)

    for h in range(heads):
        feats = products(proj[h * width:h * width + FEAT].astype(F32), 0.25, 1.0 / 32, 1.0 / 16, 0.125)
        for d in range(1, n_req):
            remote(sel.at[d, h], sel_recv.at[d, h], sel_s.at[d, h], sel_r.at[d, h], (z, rho, y)).wait_recv()
        state_h = sel[0, h].astype(F32)
        for d in range(1, n_req):
            state_h += sel_recv[d, h].astype(F32)
        att = inner[h] + jnp.dot(state_h.T.astype(BF), feats, preferred_element_type=F32)
        att = jnp.where(active, att, 0.0)
        inv = lax.rsqrt(jnp.mean(att * att, axis=0, keepdims=True) + epsilon)
        normed = (att * inv * gain_c[h * HD:(h + 1) * HD, 0:1]).astype(BF)
        for j in range(halves):
            nrm[0, h, j] = normed[:, j * tr:(j + 1) * tr]
        for d in range(1, n_col):
            send(nrm.at[0, h], nrm.at[d, h], nrm_s.at[d, h], nrm_r.at[d, h], (z, rho, (y + d) % n_col))
        scatter(0, h)
        if h > 0:
            pass_on(h - 1)
    pass_on(heads - 1)
    total = jnp.dot(wo_t[...], hid[rho], preferred_element_type=F32)
    for slot in range(1, n_row):
        src = slot_row(slot)
        if slot % 2:
            arrived(wo_all, wo_s, wo_r, slot)
        for h in range(heads):
            cols = pl.ds(h * HD, HD)
            remote(nrm.at[0, h, 0], hid.at[src, cols], hid_s.at[0, h, 0], hid_r.at[src, h], (z, rho, y)).wait_recv()
        total += jnp.dot(wo_all[slot], hid[src], preferred_element_type=F32)
    out_ref[...] = total

    for copy in sent:
        copy.wait_send()
    for slot in range(n_row):
        g, _, copy = part_copy(slot)

        @pl.when(g != y)
        def _():
            copy.wait_send()
    for d in range(n_col):
        for h in range(heads):
            for j in range(halves):
                row, copy = hid_copy(d, h, j)

                @pl.when(row != rho)
                def _():
                    copy.wait_send()


def shards(dims, tokens, qkv_weight, out_weight, head_gain, prefix_keys, prefix_values, suffix_len, prefix_owner):
    n_req, n_row, n_col = dims
    dk, tr = tokens.shape
    rows, wide = out_weight.shape
    heads = rows // HD
    halves = SLOTS // tr
    qkv = qkv_weight.shape[1]
    n_pref, _, t_len = prefix_keys.shape
    vm = pltpu.VMEM
    dma = pltpu.SemaphoreType.DMA
    scratch = [
        vm((dk, tr), BF), vm((rows, wide), BF), vm((rows, 8), F32), vm((heads, HD, SLOTS), F32),
        vm((n_row, dk, tr), BF), vm((n_row, wide, rows), BF), vm((qkv, dk), BF), vm((wide, rows), BF),
        vm((heads, n_pref, FEAT, t_len), BF), vm((heads, n_pref, HD, t_len), BF),
        vm((halves, qkv, tr), BF), vm((n_row, qkv, tr), BF), vm((n_col, halves, qkv, tr), BF), vm((qkv, SLOTS), BF),
        vm((heads, n_pref, NF, HD), BF), vm((n_col, heads, n_pref, NF, HD), BF),
        vm((n_req, heads, NF, HD), BF), vm((n_req, heads, NF, HD), BF), vm((n_req, 8, 128), jnp.int32),
        vm((n_col, heads, halves, HD, tr), BF), vm((n_row, rows, tr), BF),
        dma((3,)), dma((heads,)), dma((heads,)), dma((n_row,)), dma((n_row,)), dma((n_row,)), dma((n_row,)),
        dma((n_row,)), dma((n_col, halves)), dma((n_col, heads)), dma((n_col, heads)),
        dma((n_req, heads)), dma((n_req, heads)), dma((n_req,)), dma((n_req,)),
        dma((n_col, heads)), dma((n_col, heads)), dma((n_col, heads, halves)), dma((n_row, heads)),
    ]
    here = pl.BlockSpec(memory_space=pltpu.VMEM)
    far = pl.BlockSpec(memory_space=pl.ANY)
    scalar = pl.BlockSpec(memory_space=pltpu.SMEM)
    mixed = pl.pallas_call(
        functools.partial(body, dims),
        out_shape=jax.ShapeDtypeStruct(tokens.shape, F32),
        in_specs=[far, far, far, here, far, far, scalar, scalar],
        out_specs=here,
        scratch_shapes=scratch,
        compiler_params=pltpu.CompilerParams(collective_id=0, has_side_effects=True,
                                             vmem_limit_bytes=60 * 1024 * 1024),
    )(tokens, qkv_weight.T, out_weight, head_gain[None, :], prefix_keys, prefix_values, suffix_len, prefix_owner)
    return (tokens.astype(F32) + mixed).astype(BF)


def solution(mesh):
    in_specs = (
        P("col", ("req", "row")),
        P("col", "row"),
        P("row", "col"),
        P("row"),
        P("req", "row", "col"),
        P("req", "row", "col"),
        P(("req", "col")),
        P(("req", "col")),
    )
    out_specs = P("col", ("req", "row"))
    dims = (mesh.shape["req"], mesh.shape["row"], mesh.shape["col"])
    return jax.shard_map(functools.partial(shards, dims), mesh=mesh, in_specs=in_specs, out_specs=out_specs,
                         check_vma=False)
```

```python
import functools

import jax
import jax.numpy as jnp
from jax import lax
from jax.experimental import pallas as pl
from jax.experimental.pallas import tpu as pltpu
from jax.sharding import PartitionSpec as P

FEAT = 16
SLOTS = 512
HD = 112
NF = 160
epsilon = 1e-05
MESH = pl.DeviceIdType.MESH
BF = jnp.bfloat16
F32 = jnp.float32


def products(u, linear, diag, cross, const):
    parts = [(u * linear).astype(BF), (u * u * diag).astype(BF)]
    left = u * cross
    for s in range(1, 8):
        parts.append((left * pltpu.roll(u, s, 0)).astype(BF))
    last = jnp.concatenate([left[:8] * u[8:], jnp.full((8, u.shape[1]), const, F32)], axis=0)
    parts.append(last.astype(BF))
    return jnp.concatenate(parts, axis=0)


def key_products(rows):
    u = rows.astype(F32)
    parts = [rows, rows * rows]
    for s in range(1, 8):
        parts.append(rows * pltpu.roll(u, s, 0).astype(BF))
    last = jnp.concatenate([u[:8] * u[8:], jnp.full((8, u.shape[1]), 1.0, F32)], axis=0)
    parts.append(last.astype(BF))
    return jnp.concatenate(parts, axis=0)


def body(dims, tok_any, qkv_any, wo_any, gain_ref, keys_ref, vals_ref, len_ref, own_ref, out_ref,
         tok_ref, wo_ref, gain_c, inner, tok_all, wo_all, qkv_t, wo_t, keys_v, vals_v, own_part, send_part, recv_part, proj,
         st_part, st_recv, sel, sel_recv, own_all, nrm, hid,
         ld_w, ld_k, ld_v, tok_s, tok_r, wo_s, wo_r, part_s, part_r, st_s, st_r, sel_s, sel_r, ow_s, ow_r,
         nrm_s, nrm_r, hid_s, hid_r):
    n_req, n_row, n_col = dims
    n_x = n_row // 2
    z, rho, y = lax.axis_index("req"), lax.axis_index("row"), lax.axis_index("col")
    x, c = rho // 2, rho % 2
    mate = x * 2 + (1 - c)
    heads = gain_c.shape[0] // HD
    b = z % 2
    z_mate = z - b + 1 - b
    width = 2 * FEAT + HD
    tr = tok_ref.shape[1]
    halves = SLOTS // tr
    n_pref, _, t_len = keys_ref.shape

    first = [pltpu.make_async_copy(tok_any, tok_ref, ld_w.at[0]),
             pltpu.make_async_copy(qkv_any, qkv_t, ld_w.at[1]),
             pltpu.make_async_copy(wo_any, wo_ref, ld_w.at[2])]
    first[0].start()
    first[1].start()
    first[2].start()
    loads = []
    for h in range(heads):
        pair = (pltpu.make_async_copy(keys_ref.at[:, pl.ds(h * FEAT, FEAT)], keys_v.at[h], ld_k.at[h]),
                pltpu.make_async_copy(vals_ref.at[:, pl.ds(h * HD, HD)], vals_v.at[h], ld_v.at[h]))
        pair[0].start()
        pair[1].start()
        loads.append(pair)

    barrier = pltpu.get_barrier_semaphore()
    for d in range(1, n_row):
        pl.semaphore_signal(barrier, inc=1, device_id=(z, (rho + d) % n_row, y), device_id_type=MESH)
    for d in range(1, n_col):
        pl.semaphore_signal(barrier, inc=1, device_id=(z, rho, (y + d) % n_col), device_id_type=MESH)
    for d in range(1, n_req):
        pl.semaphore_signal(barrier, inc=1, device_id=((z + d) % n_req, rho, y), device_id_type=MESH)

    own_all[0] = jnp.full((8, 128), own_ref[0], jnp.int32)
    gain_c[...] = jnp.broadcast_to(gain_ref[...], (8, gain_ref.shape[1])).T
    first[2].wait()
    first[0].wait()
    pl.semaphore_wait(barrier, n_row + n_col + n_req - 3)

    def remote(src, dst, s, r, dev):
        return pltpu.make_async_remote_copy(src_ref=src, dst_ref=dst, send_sem=s, recv_sem=r,
                                            device_id=dev, device_id_type=MESH)

    sent = []

    def send(*args):
        copy = remote(*args)
        copy.start()
        sent.append(copy)

    def forward(dst, ss, rs, d):
        remote(dst.at[2 * d], dst.at[2 * d], ss.at[2 * d], rs.at[2 * d], (z, mate, y)).wait_recv()
        send(dst.at[2 * d], dst.at[2 * d + 1], ss.at[2 * d + 1], rs.at[2 * d + 1], (z, mate, y))

    def wo_came(slot, part, way):
        remote(wo_all.at[slot, part], wo_all.at[slot, part], wo_s.at[slot, way], wo_r.at[slot, way],
               (z, mate, y)).wait_recv()

    def wo_send(slot, part, way, to, dev):
        send(wo_all.at[slot, part], wo_all.at[to, part], wo_s.at[to, way], wo_r.at[to, way], dev)

    def turn(slot):
        half_rows = wo_ref.shape[1]
        for i in range(2):
            wo_t[slot, :, i * half_rows:(i + 1) * half_rows] = (wo_ref[i] if slot == 0 else wo_all[slot, i]).T

    def arrived(dst, ss, rs, slot):
        remote(dst.at[slot], dst.at[slot], ss.at[slot], rs.at[slot], (z, mate, y)).wait_recv()

    def slot_row(slot):
        d, s = slot // 2, slot % 2
        return ((x - d + n_x) % n_x) * 2 + (c if s == 0 else 1 - c)

    for d in range(1, n_x):
        send(tok_ref, tok_all.at[2 * d], tok_s.at[2 * d], tok_r.at[2 * d], (z, ((x + d) % n_x) * 2 + c, y))
    send(tok_ref, tok_all.at[1], tok_s.at[1], tok_r.at[1], (z, mate, y))
    for d in range(1, n_req):
        send(own_all.at[0], own_all.at[d], ow_s.at[d], ow_r.at[d], ((z + d) % n_req, rho, y))

    def part_copy(slot):
        row = slot_row(slot)
        g = row * tr // SLOTS
        j = row % halves
        d = (g - y + n_col) % n_col
        k = (d - 1 + n_col) % n_col
        return g, j, remote(send_part.at[slot], recv_part.at[k, j], part_s.at[slot], part_r.at[k, j], (z, rho, g))

    def project(slot):
        tokens = tok_ref[...] if slot == 0 else tok_all[slot]
        value = jnp.dot(qkv_t[...], tokens, preferred_element_type=F32).astype(BF)
        g, j, copy = part_copy(slot)

        @pl.when(g == y)
        def _():
            own_part[j] = value

        @pl.when(g != y)
        def _():
            send_part[slot] = value
            copy.start()

    first[1].wait()
    project(0)
    arrived(tok_all, tok_s, tok_r, 1)
    project(1)
    send(wo_ref, wo_all.at[1], wo_s.at[1, 0], wo_r.at[1, 0], (z, mate, y))

    step = min(1024, t_len)

    def state(h):
        loads[h][0].wait()
        loads[h][1].wait()

        def one(p, carry):
            total = jnp.zeros((NF, HD), F32)
            for t in range(0, t_len, step):
                feats = key_products(keys_v[h, p, :, t:t + step])
                total += lax.dot_general(feats, vals_v[h, p, :, t:t + step], (((1,), (1,)), ((), ())),
                                         preferred_element_type=F32)
            st_part[h, p] = total.astype(BF)
            return carry

        lax.fori_loop(0, n_pref, one, 0)
        for d in range(1, n_col):
            send(st_part.at[h], st_recv.at[d, h], st_s.at[d, h], st_r.at[d, h], (z, rho, (y + d) % n_col))

    def choose(h):
        if h == 0:
            for d in range(1, n_req):
                remote(own_all.at[0], own_all.at[d], ow_s.at[d], ow_r.at[d], (z, rho, y)).wait_recv()
        for d in range(1, n_col):
            remote(st_part.at[h], st_recv.at[d, h], st_s.at[d, h], st_r.at[d, h], (z, rho, y)).wait_recv()
        sums = []
        for p in range(n_pref):
            total = st_part[h, p].astype(F32)
            for d in range(1, n_col):
                total += st_recv[d, h, p].astype(F32)
            sums.append(total)
        for d in list(range(1, n_req)) + [0]:
            k = (n_req - d) % n_req
            owner = own_all[k, 0:1, 0:HD]
            value = jnp.zeros((NF, HD), F32)
            for p in range(n_pref):
                value = jnp.where(owner == z * n_pref + p, sums[p], value)
            sel[d, h] = value.astype(BF)
            if d:
                send(sel.at[d, h], sel_recv.at[d, h], sel_s.at[d, h], sel_r.at[d, h], ((z + d) % n_req, rho, y))

    half = max(1, heads // 2)
    for h in range(heads):
        state(h)
        if h > 0:
            choose(h - 1)
        if h == half - 1:
            for d in range(1, n_x):
                forward(tok_all, tok_s, tok_r, d)
                send(wo_ref.at[b], wo_all.at[2 * d, b], wo_s.at[2 * d, 0], wo_r.at[2 * d, 0],
                     (z, ((x + d) % n_x) * 2 + c, y))
                project(2 * d)
        if h == half:
            for d in range(1, n_x):
                arrived(tok_all, tok_s, tok_r, 2 * d + 1)
                project(2 * d + 1)
    choose(heads - 1)
    turn(0)
    remote(wo_ref, wo_all.at[1], wo_s.at[1, 0], wo_r.at[1, 0], (z, mate, y)).wait_recv()
    turn(1)
    for d in range(1, n_x):
        wo_came(2 * d, b, 0)
        wo_send(2 * d, b, 1, 2 * d, (z_mate, rho, y))
        wo_send(2 * d, b, 0, 2 * d + 1, (z, mate, y))

    for j in range(halves):
        total = own_part[j].astype(F32)
        for d in range(1, n_col):
            k = d - 1
            remote(send_part.at[0], recv_part.at[k, j], part_s.at[0], part_r.at[k, j], (z, rho, y)).wait_recv()
            total += recv_part[k, j].astype(F32)
        proj[:, j * tr:(j + 1) * tr] = total.astype(BF)

    def hid_copy(d, h, j):
        row = ((y - d + n_col) % n_col) * halves + j
        cols = pl.ds(h * HD, HD)
        return row, remote(nrm.at[d, h, j], hid.at[rho, cols], hid_s.at[d, h, j], hid_r.at[rho, h], (z, row, y))

    def scatter(d, h):
        for j in range(halves):
            row, copy = hid_copy(d, h, j)

            @pl.when(row == rho)
            def _():
                hid[rho, h * HD:(h + 1) * HD] = nrm[d, h, j]

            @pl.when(row != rho)
            def _():
                copy.start()

    def pass_on(h):
        for d in range(1, n_col):
            remote(nrm.at[0, h], nrm.at[d, h], nrm_s.at[d, h], nrm_r.at[d, h], (z, rho, y)).wait_recv()
            scatter(d, h)

    tile = min(tr, 256)
    live = len_ref[0]
    active = lax.broadcasted_iota(jnp.int32, (HD, SLOTS), 1) < live
    for h in range(heads):
        base = h * width
        q = proj[base:base + FEAT]
        k_rows = proj[base + FEAT:base + 2 * FEAT].astype(F32).T.astype(BF)
        v = proj[base + 2 * FEAT:base + width]
        v = jnp.where(active, v.astype(F32), 0.0).astype(BF)
        for t in range(0, SLOTS, tile):
            keep = t + tile
            scores = jnp.dot(k_rows[:keep], q[:, t:keep], preferred_element_type=F32)
            weights = 1.0 + scores * 0.25 + scores * scores * (0.5 / FEAT)
            si = lax.broadcasted_iota(jnp.int32, (keep, tile), 0)
            ti = lax.broadcasted_iota(jnp.int32, (keep, tile), 1) + t
            weights = jnp.where(si <= ti, weights, 0.0).astype(BF)
            inner[h, :, t:keep] = jnp.dot(v[:, :keep], weights, preferred_element_type=F32)

    for h in range(heads):
        feats = products(proj[h * width:h * width + FEAT].astype(F32), 0.25, 1.0 / 32, 1.0 / 16, 0.125)
        for d in range(1, n_req):
            remote(sel.at[d, h], sel_recv.at[d, h], sel_s.at[d, h], sel_r.at[d, h], (z, rho, y)).wait_recv()
        state_h = sel[0, h].astype(F32)
        for d in range(1, n_req):
            state_h += sel_recv[d, h].astype(F32)
        att = inner[h] + jnp.dot(state_h.T.astype(BF), feats, preferred_element_type=F32)
        att = jnp.where(active, att, 0.0)
        inv = lax.rsqrt(jnp.mean(att * att, axis=0, keepdims=True) + epsilon)
        normed = (att * inv * gain_c[h * HD:(h + 1) * HD, 0:1]).astype(BF)
        for j in range(halves):
            nrm[0, h, j] = normed[:, j * tr:(j + 1) * tr]
        for d in range(1, n_col):
            send(nrm.at[0, h], nrm.at[d, h], nrm_s.at[d, h], nrm_r.at[d, h], (z, rho, (y + d) % n_col))
        scatter(0, h)
        if h > 0:
            pass_on(h - 1)
    for d in range(1, n_x):
        wo_came(2 * d, 1 - b, 1)
        wo_send(2 * d, 1 - b, 1, 2 * d + 1, (z, mate, y))
        turn(2 * d)
    pass_on(heads - 1)
    for d in range(1, n_x):
        wo_came(2 * d + 1, b, 0)
        wo_came(2 * d + 1, 1 - b, 1)
        turn(2 * d + 1)
    total = jnp.dot(wo_t[0], hid[rho], preferred_element_type=F32)
    for slot in range(1, n_row):
        src = slot_row(slot)
        for h in range(heads):
            cols = pl.ds(h * HD, HD)
            remote(nrm.at[0, h, 0], hid.at[src, cols], hid_s.at[0, h, 0], hid_r.at[src, h], (z, rho, y)).wait_recv()
        total += jnp.dot(wo_t[slot], hid[src], preferred_element_type=F32)
    out_ref[...] = total

    for copy in sent:
        copy.wait_send()
    for slot in range(n_row):
        g, _, copy = part_copy(slot)

        @pl.when(g != y)
        def _():
            copy.wait_send()
    for d in range(n_col):
        for h in range(heads):
            for j in range(halves):
                row, copy = hid_copy(d, h, j)

                @pl.when(row != rho)
                def _():
                    copy.wait_send()


def shards(dims, tokens, qkv_weight, out_weight, head_gain, prefix_keys, prefix_values, suffix_len, prefix_owner):
    n_req, n_row, n_col = dims
    dk, tr = tokens.shape
    rows, wide = out_weight.shape
    heads = rows // HD
    halves = SLOTS // tr
    qkv = qkv_weight.shape[1]
    n_pref, _, t_len = prefix_keys.shape
    vm = pltpu.VMEM
    dma = pltpu.SemaphoreType.DMA
    scratch = [
        vm((dk, tr), BF), vm((2, rows // 2, wide), BF), vm((rows, 8), F32), vm((heads, HD, SLOTS), F32),
        vm((n_row, dk, tr), BF), vm((n_row, 2, rows // 2, wide), BF), vm((qkv, dk), BF), vm((n_row, wide, rows), BF),
        vm((heads, n_pref, FEAT, t_len), BF), vm((heads, n_pref, HD, t_len), BF),
        vm((halves, qkv, tr), BF), vm((n_row, qkv, tr), BF), vm((n_col, halves, qkv, tr), BF), vm((qkv, SLOTS), BF),
        vm((heads, n_pref, NF, HD), BF), vm((n_col, heads, n_pref, NF, HD), BF),
        vm((n_req, heads, NF, HD), BF), vm((n_req, heads, NF, HD), BF), vm((n_req, 8, 128), jnp.int32),
        vm((n_col, heads, halves, HD, tr), BF), vm((n_row, rows, tr), BF),
        dma((3,)), dma((heads,)), dma((heads,)), dma((n_row,)), dma((n_row,)), dma((n_row, 2)), dma((n_row, 2)),
        dma((n_row,)), dma((n_col, halves)), dma((n_col, heads)), dma((n_col, heads)),
        dma((n_req, heads)), dma((n_req, heads)), dma((n_req,)), dma((n_req,)),
        dma((n_col, heads)), dma((n_col, heads)), dma((n_col, heads, halves)), dma((n_row, heads)),
    ]
    here = pl.BlockSpec(memory_space=pltpu.VMEM)
    far = pl.BlockSpec(memory_space=pl.ANY)
    scalar = pl.BlockSpec(memory_space=pltpu.SMEM)
    mixed = pl.pallas_call(
        functools.partial(body, dims),
        out_shape=jax.ShapeDtypeStruct(tokens.shape, F32),
        in_specs=[far, far, far, here, far, far, scalar, scalar],
        out_specs=here,
        scratch_shapes=scratch,
        compiler_params=pltpu.CompilerParams(collective_id=0, has_side_effects=True,
                                             vmem_limit_bytes=60 * 1024 * 1024),
    )(tokens, qkv_weight.T, out_weight.reshape(2, rows // 2, wide), head_gain[None, :], prefix_keys, prefix_values, suffix_len, prefix_owner)
    return (tokens.astype(F32) + mixed).astype(BF)


def solution(mesh):
    in_specs = (
        P("col", ("req", "row")),
        P("col", "row"),
        P("row", "col"),
        P("row"),
        P("req", "row", "col"),
        P("req", "row", "col"),
        P(("req", "col")),
        P(("req", "col")),
    )
    out_specs = P("col", ("req", "row"))
    dims = (mesh.shape["req"], mesh.shape["row"], mesh.shape["col"])
    return jax.shard_map(functools.partial(shards, dims), mesh=mesh, in_specs=in_specs, out_specs=out_specs,
                         check_vma=False)
```

```python
import functools

import jax
import jax.numpy as jnp
from jax import lax
from jax.experimental import pallas as pl
from jax.experimental.pallas import tpu as pltpu
from jax.sharding import PartitionSpec as P

FEAT = 16
SLOTS = 512
HD = 112
NF = 160
epsilon = 1e-05
MESH = pl.DeviceIdType.MESH
BF = jnp.bfloat16
F32 = jnp.float32


def products(u, linear, diag, cross, const):
    parts = [(u * linear).astype(BF), (u * u * diag).astype(BF)]
    left = u * cross
    for s in range(1, 8):
        rolled = jnp.concatenate([u[s:], u[:s]], axis=0)
        parts.append((left * rolled).astype(BF))
    last = jnp.concatenate([left[:8] * u[8:], jnp.full((8, u.shape[1]), const, F32)], axis=0)
    parts.append(last.astype(BF))
    return jnp.concatenate(parts, axis=0)


def body(dims, tok_any, qkv_any, wo_any, gain_ref, keys_ref, vals_ref, len_ref, own_ref, out_ref,
         tok_ref, wo_ref, gain_c, inner, tok_all, wo_all, qkv_t, wo_t, keys_v, vals_v, own_part, send_part, recv_part, proj,
         st_part, st_recv, sel, sel_recv, own_all, nrm, hid,
         ld_w, ld_k, ld_v, tok_s, tok_r, wo_s, wo_r, part_s, part_r, st_s, st_r, sel_s, sel_r, ow_s, ow_r,
         nrm_s, nrm_r, hid_s, hid_r):
    n_req, n_row, n_col = dims
    n_x = n_row // 2
    z, rho, y = lax.axis_index("req"), lax.axis_index("row"), lax.axis_index("col")
    x, c = rho // 2, rho % 2
    mate = x * 2 + (1 - c)
    heads = gain_c.shape[0] // HD
    b = z % 2
    z_mate = z - b + 1 - b
    width = 2 * FEAT + HD
    tr = tok_ref.shape[1]
    halves = SLOTS // tr
    n_pref, _, t_len = keys_ref.shape

    first = [pltpu.make_async_copy(tok_any, tok_ref, ld_w.at[0]),
             pltpu.make_async_copy(qkv_any, qkv_t, ld_w.at[1]),
             pltpu.make_async_copy(wo_any, wo_ref, ld_w.at[2])]
    first[0].start()
    first[1].start()
    first[2].start()
    loads = []
    for h in range(heads):
        pair = (pltpu.make_async_copy(keys_ref.at[:, pl.ds(h * FEAT, FEAT)], keys_v.at[h], ld_k.at[h]),
                pltpu.make_async_copy(vals_ref.at[:, pl.ds(h * HD, HD)], vals_v.at[h], ld_v.at[h]))
        pair[0].start()
        pair[1].start()
        loads.append(pair)

    barrier = pltpu.get_barrier_semaphore()
    for d in range(1, n_row):
        pl.semaphore_signal(barrier, inc=1, device_id=(z, (rho + d) % n_row, y), device_id_type=MESH)
    for d in range(1, n_col):
        pl.semaphore_signal(barrier, inc=1, device_id=(z, rho, (y + d) % n_col), device_id_type=MESH)
    for d in range(1, n_req):
        pl.semaphore_signal(barrier, inc=1, device_id=((z + d) % n_req, rho, y), device_id_type=MESH)

    own_all[0] = jnp.full((8, 128), own_ref[0], jnp.int32)
    gain_c[...] = jnp.broadcast_to(gain_ref[...], (8, gain_ref.shape[1])).T
    first[2].wait()
    first[0].wait()
    pl.semaphore_wait(barrier, n_row + n_col + n_req - 3)

    def remote(src, dst, s, r, dev):
        return pltpu.make_async_remote_copy(src_ref=src, dst_ref=dst, send_sem=s, recv_sem=r,
                                            device_id=dev, device_id_type=MESH)

    sent = []

    def send(*args):
        copy = remote(*args)
        copy.start()
        sent.append(copy)

    def forward(dst, ss, rs, d):
        remote(dst.at[2 * d], dst.at[2 * d], ss.at[2 * d], rs.at[2 * d], (z, mate, y)).wait_recv()
        send(dst.at[2 * d], dst.at[2 * d + 1], ss.at[2 * d + 1], rs.at[2 * d + 1], (z, mate, y))

    def wo_came(slot, part, way):
        remote(wo_all.at[slot, part], wo_all.at[slot, part], wo_s.at[slot, way], wo_r.at[slot, way],
               (z, mate, y)).wait_recv()

    def wo_send(slot, part, way, to, dev):
        send(wo_all.at[slot, part], wo_all.at[to, part], wo_s.at[to, way], wo_r.at[to, way], dev)

    def turn(slot):
        half_rows = wo_ref.shape[1]
        for i in range(2):
            wo_t[slot, :, i * half_rows:(i + 1) * half_rows] = (wo_ref[i] if slot == 0 else wo_all[slot, i]).T

    def arrived(dst, ss, rs, slot):
        remote(dst.at[slot], dst.at[slot], ss.at[slot], rs.at[slot], (z, mate, y)).wait_recv()

    def slot_row(slot):
        d, s = slot // 2, slot % 2
        return ((x - d + n_x) % n_x) * 2 + (c if s == 0 else 1 - c)

    for d in range(1, n_x):
        send(tok_ref, tok_all.at[2 * d], tok_s.at[2 * d], tok_r.at[2 * d], (z, ((x + d) % n_x) * 2 + c, y))
    send(tok_ref, tok_all.at[1], tok_s.at[1], tok_r.at[1], (z, mate, y))
    for d in range(1, n_req):
        send(own_all.at[0], own_all.at[d], ow_s.at[d], ow_r.at[d], ((z + d) % n_req, rho, y))

    def part_copy(slot):
        row = slot_row(slot)
        g = row * tr // SLOTS
        j = row % halves
        d = (g - y + n_col) % n_col
        k = (d - 1 + n_col) % n_col
        return g, j, remote(send_part.at[slot], recv_part.at[k, j], part_s.at[slot], part_r.at[k, j], (z, rho, g))

    def project(slot):
        tokens = tok_ref[...] if slot == 0 else tok_all[slot]
        value = jnp.dot(qkv_t[...], tokens, preferred_element_type=F32).astype(BF)
        g, j, copy = part_copy(slot)

        @pl.when(g == y)
        def _():
            own_part[j] = value

        @pl.when(g != y)
        def _():
            send_part[slot] = value
            copy.start()

    first[1].wait()
    project(0)
    arrived(tok_all, tok_s, tok_r, 1)
    project(1)
    send(wo_ref, wo_all.at[1], wo_s.at[1, 0], wo_r.at[1, 0], (z, mate, y))

    step = min(1024, t_len)

    def state(h):
        loads[h][0].wait()
        loads[h][1].wait()

        def one(p, carry):
            total = jnp.zeros((NF, HD), F32)
            for t in range(0, t_len, step):
                feats = products(keys_v[h, p, :, t:t + step].astype(F32), 1.0, 1.0, 1.0, 1.0)
                total += lax.dot_general(feats, vals_v[h, p, :, t:t + step], (((1,), (1,)), ((), ())),
                                         preferred_element_type=F32)
            st_part[h, p] = total.astype(BF)
            return carry

        lax.fori_loop(0, n_pref, one, 0)
        for d in range(1, n_col):
            send(st_part.at[h], st_recv.at[d, h], st_s.at[d, h], st_r.at[d, h], (z, rho, (y + d) % n_col))

    def choose(h):
        if h == 0:
            for d in range(1, n_req):
                remote(own_all.at[0], own_all.at[d], ow_s.at[d], ow_r.at[d], (z, rho, y)).wait_recv()
        for d in range(1, n_col):
            remote(st_part.at[h], st_recv.at[d, h], st_s.at[d, h], st_r.at[d, h], (z, rho, y)).wait_recv()
        sums = []
        for p in range(n_pref):
            total = st_part[h, p].astype(F32)
            for d in range(1, n_col):
                total += st_recv[d, h, p].astype(F32)
            sums.append(total)
        for d in list(range(1, n_req)) + [0]:
            k = (n_req - d) % n_req
            owner = own_all[k, 0:1, 0:HD]
            value = jnp.zeros((NF, HD), F32)
            for p in range(n_pref):
                value = jnp.where(owner == z * n_pref + p, sums[p], value)
            sel[d, h] = value.astype(BF)
            if d:
                send(sel.at[d, h], sel_recv.at[d, h], sel_s.at[d, h], sel_r.at[d, h], ((z + d) % n_req, rho, y))

    half = max(1, heads // 2)
    for h in range(heads):
        state(h)
        if h > 0:
            choose(h - 1)
        if h == half - 1:
            for d in range(1, n_x):
                forward(tok_all, tok_s, tok_r, d)
                send(wo_ref.at[b], wo_all.at[2 * d, b], wo_s.at[2 * d, 0], wo_r.at[2 * d, 0],
                     (z, ((x + d) % n_x) * 2 + c, y))
                project(2 * d)
        if h == half:
            for d in range(1, n_x):
                arrived(tok_all, tok_s, tok_r, 2 * d + 1)
                project(2 * d + 1)
    choose(heads - 1)
    turn(0)
    remote(wo_ref, wo_all.at[1], wo_s.at[1, 0], wo_r.at[1, 0], (z, mate, y)).wait_recv()
    turn(1)
    for d in range(1, n_x):
        wo_came(2 * d, b, 0)
        wo_send(2 * d, b, 1, 2 * d, (z_mate, rho, y))
        wo_send(2 * d, b, 0, 2 * d + 1, (z, mate, y))

    for j in range(halves):
        total = own_part[j].astype(F32)
        for d in range(1, n_col):
            k = d - 1
            remote(send_part.at[0], recv_part.at[k, j], part_s.at[0], part_r.at[k, j], (z, rho, y)).wait_recv()
            total += recv_part[k, j].astype(F32)
        proj[:, j * tr:(j + 1) * tr] = total.astype(BF)

    def hid_copy(d, h, j):
        row = ((y - d + n_col) % n_col) * halves + j
        cols = pl.ds(h * HD, HD)
        return row, remote(nrm.at[d, h, j], hid.at[rho, cols], hid_s.at[d, h, j], hid_r.at[rho, h], (z, row, y))

    def scatter(d, h):
        for j in range(halves):
            row, copy = hid_copy(d, h, j)

            @pl.when(row == rho)
            def _():
                hid[rho, h * HD:(h + 1) * HD] = nrm[d, h, j]

            @pl.when(row != rho)
            def _():
                copy.start()

    def pass_on(h):
        for d in range(1, n_col):
            remote(nrm.at[0, h], nrm.at[d, h], nrm_s.at[d, h], nrm_r.at[d, h], (z, rho, y)).wait_recv()
            scatter(d, h)

    tile = min(tr, 256)
    live = len_ref[0]
    active = lax.broadcasted_iota(jnp.int32, (HD, SLOTS), 1) < live
    for h in range(heads):
        base = h * width
        q = proj[base:base + FEAT]
        k_rows = proj[base + FEAT:base + 2 * FEAT].astype(F32).T.astype(BF)
        v = proj[base + 2 * FEAT:base + width]
        v = jnp.where(active, v.astype(F32), 0.0).astype(BF)
        for t in range(0, SLOTS, tile):
            keep = t + tile
            scores = jnp.dot(k_rows[:keep], q[:, t:keep], preferred_element_type=F32)
            weights = 1.0 + scores * 0.25 + scores * scores * (0.5 / FEAT)
            si = lax.broadcasted_iota(jnp.int32, (keep, tile), 0)
            ti = lax.broadcasted_iota(jnp.int32, (keep, tile), 1) + t
            weights = jnp.where(si <= ti, weights, 0.0).astype(BF)
            inner[h, :, t:keep] = jnp.dot(v[:, :keep], weights, preferred_element_type=F32)

    for h in range(heads):
        feats = products(proj[h * width:h * width + FEAT].astype(F32), 0.25, 1.0 / 32, 1.0 / 16, 0.125)
        for d in range(1, n_req):
            remote(sel.at[d, h], sel_recv.at[d, h], sel_s.at[d, h], sel_r.at[d, h], (z, rho, y)).wait_recv()
        state_h = sel[0, h].astype(F32)
        for d in range(1, n_req):
            state_h += sel_recv[d, h].astype(F32)
        att = inner[h] + jnp.dot(state_h.T.astype(BF), feats, preferred_element_type=F32)
        att = jnp.where(active, att, 0.0)
        inv = lax.rsqrt(jnp.mean(att * att, axis=0, keepdims=True) + epsilon)
        normed = (att * inv * gain_c[h * HD:(h + 1) * HD, 0:1]).astype(BF)
        for j in range(halves):
            nrm[0, h, j] = normed[:, j * tr:(j + 1) * tr]
        for d in range(1, n_col):
            send(nrm.at[0, h], nrm.at[d, h], nrm_s.at[d, h], nrm_r.at[d, h], (z, rho, (y + d) % n_col))
        scatter(0, h)
        if h > 0:
            pass_on(h - 1)
    for d in range(1, n_x):
        wo_came(2 * d, 1 - b, 1)
        wo_send(2 * d, 1 - b, 1, 2 * d + 1, (z, mate, y))
        turn(2 * d)
    pass_on(heads - 1)
    for d in range(1, n_x):
        wo_came(2 * d + 1, b, 0)
        wo_came(2 * d + 1, 1 - b, 1)
        turn(2 * d + 1)
    total = jnp.dot(wo_t[0], hid[rho], preferred_element_type=F32)
    for slot in range(1, n_row):
        src = slot_row(slot)
        for h in range(heads):
            cols = pl.ds(h * HD, HD)
            remote(nrm.at[0, h, 0], hid.at[src, cols], hid_s.at[0, h, 0], hid_r.at[src, h], (z, rho, y)).wait_recv()
        total += jnp.dot(wo_t[slot], hid[src], preferred_element_type=F32)
    out_ref[...] = total

    for copy in sent:
        copy.wait_send()
    for slot in range(n_row):
        g, _, copy = part_copy(slot)

        @pl.when(g != y)
        def _():
            copy.wait_send()
    for d in range(n_col):
        for h in range(heads):
            for j in range(halves):
                row, copy = hid_copy(d, h, j)

                @pl.when(row != rho)
                def _():
                    copy.wait_send()


def shards(dims, tokens, qkv_weight, out_weight, head_gain, prefix_keys, prefix_values, suffix_len, prefix_owner):
    n_req, n_row, n_col = dims
    dk, tr = tokens.shape
    rows, wide = out_weight.shape
    heads = rows // HD
    halves = SLOTS // tr
    qkv = qkv_weight.shape[1]
    n_pref, _, t_len = prefix_keys.shape
    vm = pltpu.VMEM
    dma = pltpu.SemaphoreType.DMA
    scratch = [
        vm((dk, tr), BF), vm((2, rows // 2, wide), BF), vm((rows, 8), F32), vm((heads, HD, SLOTS), F32),
        vm((n_row, dk, tr), BF), vm((n_row, 2, rows // 2, wide), BF), vm((qkv, dk), BF), vm((n_row, wide, rows), BF),
        vm((heads, n_pref, FEAT, t_len), BF), vm((heads, n_pref, HD, t_len), BF),
        vm((halves, qkv, tr), BF), vm((n_row, qkv, tr), BF), vm((n_col, halves, qkv, tr), BF), vm((qkv, SLOTS), BF),
        vm((heads, n_pref, NF, HD), BF), vm((n_col, heads, n_pref, NF, HD), BF),
        vm((n_req, heads, NF, HD), BF), vm((n_req, heads, NF, HD), BF), vm((n_req, 8, 128), jnp.int32),
        vm((n_col, heads, halves, HD, tr), BF), vm((n_row, rows, tr), BF),
        dma((3,)), dma((heads,)), dma((heads,)), dma((n_row,)), dma((n_row,)), dma((n_row, 2)), dma((n_row, 2)),
        dma((n_row,)), dma((n_col, halves)), dma((n_col, heads)), dma((n_col, heads)),
        dma((n_req, heads)), dma((n_req, heads)), dma((n_req,)), dma((n_req,)),
        dma((n_col, heads)), dma((n_col, heads)), dma((n_col, heads, halves)), dma((n_row, heads)),
    ]
    here = pl.BlockSpec(memory_space=pltpu.VMEM)
    far = pl.BlockSpec(memory_space=pl.ANY)
    scalar = pl.BlockSpec(memory_space=pltpu.SMEM)
    mixed = pl.pallas_call(
        functools.partial(body, dims),
        out_shape=jax.ShapeDtypeStruct(tokens.shape, F32),
        in_specs=[far, far, far, here, far, far, scalar, scalar],
        out_specs=here,
        scratch_shapes=scratch,
        compiler_params=pltpu.CompilerParams(collective_id=0, has_side_effects=True,
                                             vmem_limit_bytes=60 * 1024 * 1024),
    )(tokens, qkv_weight.T, out_weight.reshape(2, rows // 2, wide), head_gain[None, :], prefix_keys, prefix_values, suffix_len, prefix_owner)
    return (tokens.astype(F32) + mixed).astype(BF)


def solution(mesh):
    in_specs = (
        P("col", ("req", "row")),
        P("col", "row"),
        P("row", "col"),
        P("row"),
        P("req", "row", "col"),
        P("req", "row", "col"),
        P(("req", "col")),
        P(("req", "col")),
    )
    out_specs = P("col", ("req", "row"))
    dims = (mesh.shape["req"], mesh.shape["row"], mesh.shape["col"])
    return jax.shard_map(functools.partial(shards, dims), mesh=mesh, in_specs=in_specs, out_specs=out_specs,
                         check_vma=False)
```
